32 devices in a mesh: groups: 2 (over y), space: 8 (over z, x), dp: 2 (over core).
Axes of the slice: x: 2, y: 2, z: 4, core: 2. Of those that a mesh axis runs over, the one named last changes fastest.
Arguments:
- tokens: bfloat16 [8, 16, 64, 768], P('groups', 'dp', 'space'), parts along dimension 0, may hold values from -45 to 45
- cotangent: bfloat16 [8, 16, 64, 768], P('groups', 'dp', 'space'), parts along dimension 0, may hold values from -6 to 6
- region: int32 [8, 16, 64], P('groups', 'dp', 'space'), parts along dimension 0, may hold values from 0 to 3
- qkv_weight: bfloat16 [768, 2304], P(('space', 'dp')), may hold values from -0.21875 to 0.21875
- proj_weight: bfloat16 [768, 768], P(None, ('space', 'dp')), may hold values from -0.21875 to 0.21875
- logit_scale: float32 [12], replicated, may hold values from 2 to 25
Outputs:
- block_output: bfloat16 [8, 16, 64, 768], P('groups', 'dp', 'space'), parts along dimension 0
- token_grad: bfloat16 [8, 16, 64, 768], P('groups', 'dp', 'space'), parts along dimension 0
- proj_grad: float32 [1536, 768], P('groups', ('space', 'dp')), parts along dimension 0
The draws below stay inside these ranges and needn't reach their ends.
There are 2 independent parts, one for each index of `groups`. The reference program is written for one: setup_inputs(seed, part) draws one part's arguments, and reference() takes and returns one part's arrays. A program takes and returns all parts, laid end to end along the dimension named above; an argument that names none is the same for every part. Nothing has to cross between parts.
Inputs may be any that keep to these rules, and one draw needn't show every extreme that they name: region[d, h, w] labels the token that sits at position (d, h, w) of the shifted grid, that is tokens[(d + 2) mod 4, (h + 4) mod 16, (w + 4) mod 64].
All inputs are finite; a program needn't handle non-finite values.
Results may differ from the reference program's by a relative error of at most 0.012.
The reference program's roundings to bfloat16 on the way count: a program that leaves them out, or rounds other values in their place, can miss the bound.
Values may be sent and summed in bfloat16 or wider, within the bound.
A program may use at most 64 MiB of HBM per device.

```python
import math
import jax
import jax.numpy as jnp
from jax import lax

C = 768
HEADS = 12
HEAD_GROUP = 4
WD = 4
WH = 8
WW = 8
SD = 2
SH = 4
SW = 4
REGIONS = 4
DEPTH = 4
HD = 768
HEIGHT = 16
WIDTH = 64
TOKENS = 4096


def draw_tokens(key, part):
    key_base, key_row, key_col = jax.random.split(key, 3)
    full_shape = (DEPTH, HEIGHT, WIDTH, C)
    row_scale = jnp.exp(jax.random.uniform(key_row, (DEPTH, HEIGHT, WIDTH, 1), jnp.float32, math.log(0.3), math.log(3.0)))
    col_scale = jnp.exp(jax.random.uniform(key_col, (C,), jnp.float32, math.log(0.3), math.log(3.0)))
    base_draw = jnp.clip(jax.random.normal(key_base, full_shape, jnp.float32), -5.0, 5.0)
    return (base_draw * row_scale * col_scale).astype(jnp.bfloat16)


def with_ends(result, own_key, smallest, high):
    shape = result.shape
    spot = [jax.random.randint(jax.random.fold_in(own_key, axis), (), 0, shape[axis]) for axis in range(len(shape))]
    result = result.at[tuple(spot)].set(smallest)
    longest = shape.index(max(shape))
    spot[longest] = (spot[longest] + 1) % shape[longest]
    return result.at[tuple(spot)].set(high)


def strengthened(drawn, key, source, target, shards_of, factor):
    owner, partner = [(jnp.arange(drawn.shape[axis_at]) // (drawn.shape[axis_at] // shards_of)).reshape([-1 if axis == axis_at else 1 for axis in range(drawn.ndim)]) for axis_at in (source, target)]
    chosen = jax.random.permutation(key, shards_of)[partner]
    strong = (owner == chosen) | (owner == (partner + shards_of // 2) % shards_of)
    return jnp.where(strong, factor * drawn, drawn)


def shard_levels(stream_key, dims, cuts, smallest, high):
    gain = 1.0
    for dim, parts in cuts:
        heights = jax.random.uniform(jax.random.fold_in(jax.random.fold_in(stream_key, 6), dim), (parts,), jnp.float32, smallest / len(cuts), high / len(cuts))
        gain = gain * jnp.repeat(jnp.exp(heights), dims[dim] // parts).reshape((-1,) + (1,) * (len(dims) - 1 - dim))
    return gain


def normal_values(stream_key, extent, deviation, bound, cuts=(), held_as=jnp.bfloat16):
    array = jax.random.normal(stream_key, extent, jnp.float32) * deviation
    if len(cuts) > 0:
        array = shard_levels(stream_key, extent, cuts, -0.22, 0.18) * array
    return jnp.clip(array, min=-bound, max=bound).astype(held_as)


def noise_with(stream_key, extent, spread, reach, shards, heavy, kind=jnp.bfloat16):
    drawn = spread * jax.random.normal(stream_key, extent, jnp.float32)
    if shards:
        drawn = drawn * shard_levels(stream_key, extent, shards, -0.22, 0.18)
    return jnp.clip(strengthened(drawn, jax.random.fold_in(stream_key, 3), *heavy), -reach, reach).astype(kind)


def setup_inputs(seed: int = 0, part: int = 0) -> dict:
    streams_of = jax.random.split(jax.random.key(seed), 7)
    part_splits = jax.random.split(jax.random.fold_in(streams_of[6], part), 7)
    tokens = draw_tokens(jax.random.fold_in(jax.random.fold_in(streams_of[6], part), 71), part)
    cotangent = noise_with(part_splits[1], (DEPTH, HEIGHT, WIDTH, C), 1.0, 6.0, ((1, 2), (2, 8)), (2, 3, 8, 2.0))
    region = with_ends(jax.random.randint(part_splits[2], (DEPTH, HEIGHT, WIDTH), 0, REGIONS), jax.random.fold_in(part_splits[2], 1), 0, REGIONS - 1).astype(jnp.int32)
    qkv_weight = normal_values(streams_of[3], (C, 3 * HD), C ** -0.5, 0.21875, ((0, 16),))
    proj_weight = normal_values(streams_of[4], (HD, C), HD ** -0.5, 0.21875, ((1, 16),))
    logit_scale = jnp.clip(jnp.exp(jax.random.uniform(streams_of[5], (HEADS,), jnp.float32, math.log(2.0), math.log(25.0))), 2.0, 25.0)
    return dict(tokens=tokens, cotangent=cotangent, region=region, qkv_weight=qkv_weight, proj_weight=proj_weight, logit_scale=logit_scale)


def to_windows(field):
    depth_cells, height_cells, width_cells = (field.shape[0], field.shape[1], field.shape[2])
    trailing = tuple(field.shape[3:])
    blocked = field.reshape((depth_cells // WD, WD, height_cells // WH, WH, width_cells // WW, WW) + trailing)
    axes_order = (0, 2, 4, 1, 3, 5) + tuple(range(6, 6 + len(trailing)))
    return blocked.transpose(axes_order).reshape((-1, WD * WH * WW) + trailing)

def from_windows(windowed, depth_cells, height_cells, width_cells):
    trailing = tuple(windowed.shape[2:])
    blocked = windowed.reshape((depth_cells // WD, height_cells // WH, width_cells // WW, WD, WH, WW) + trailing)
    axes_order = (0, 3, 1, 4, 2, 5) + tuple(range(6, 6 + len(trailing)))
    return blocked.transpose(axes_order).reshape((depth_cells, height_cells, width_cells) + trailing)

def product(pattern, left_side, right_side):
    return jnp.einsum(pattern, left_side.astype(jnp.float32), right_side.astype(jnp.float32), preferred_element_type=jnp.float32)

def head_forward(piece_qkv, allowed, scales):
    queries = piece_qkv[:, :, :, 0].astype(jnp.float32)
    key_rows = piece_qkv[:, :, :, 1].astype(jnp.float32)
    values = piece_qkv[:, :, :, 2]
    query_inv = lax.rsqrt(lax.optimization_barrier(jnp.sum(queries * queries, axis=-1, keepdims=True)) + 1e-06)
    key_inv = lax.rsqrt(lax.optimization_barrier(jnp.sum(key_rows * key_rows, axis=-1, keepdims=True)) + 1e-06)
    query_unit = queries * query_inv
    key_unit = key_rows * key_inv
    query_low = query_unit.astype(jnp.bfloat16)
    key_low = key_unit.astype(jnp.bfloat16)
    scores = product('wqhd,wkhd->whqk', query_low, key_low) * scales[None, :, None, None]
    raised = jnp.where(allowed[:, None], jnp.exp(scores), 0.0)
    probability = raised / lax.optimization_barrier(jnp.sum(raised, axis=-1, keepdims=True))
    prob_low = probability.astype(jnp.bfloat16)
    return (query_unit, key_unit, query_inv, key_inv, query_low, key_low, values, probability, prob_low)

def window_block(windows_x, windows_g, windows_region, qkv_full, proj_full, logit_scale):
    window_count, window_size, channels = windows_x.shape
    head_count = logit_scale.shape[0]
    inner_width = proj_full.shape[0]
    head_size = inner_width // head_count
    group_count = head_count // HEAD_GROUP
    flat_rows = windows_x.reshape(window_count * window_size, channels)
    packed = jnp.dot(flat_rows, qkv_full, preferred_element_type=jnp.float32).astype(jnp.bfloat16)
    packed = packed.reshape(window_count, window_size, head_count, 3, head_size)
    allowed = windows_region[:, :, None] == windows_region[:, None, :]
    group_ids = jnp.arange(group_count, dtype=jnp.int32)

    def group_pieces(group_index):
        piece_qkv = lax.dynamic_slice_in_dim(packed, group_index * HEAD_GROUP, HEAD_GROUP, 2)
        scales = lax.dynamic_slice_in_dim(logit_scale, group_index * HEAD_GROUP, HEAD_GROUP, 0)
        return (piece_qkv, scales)

    def forward_group(group_index):
        piece_qkv, scales = group_pieces(group_index)
        outs_fwd = head_forward(piece_qkv, allowed, scales)
        return product('whqk,wkhd->wqhd', outs_fwd[8], outs_fwd[6]).astype(jnp.bfloat16)
    attended = lax.map(forward_group, group_ids)
    attended = jnp.moveaxis(attended, 0, 2).reshape(window_count * window_size, inner_width)
    mixed_rows = jnp.dot(attended, proj_full, preferred_element_type=jnp.float32)
    centered = mixed_rows - lax.optimization_barrier(jnp.mean(mixed_rows, axis=-1, keepdims=True))
    inv_dev = lax.rsqrt(lax.optimization_barrier(jnp.mean(centered * centered, axis=-1, keepdims=True)) + 1e-05)
    normed = centered * inv_dev
    branch = normed.astype(jnp.bfloat16)
    grad_in = windows_g.reshape(window_count * window_size, channels).astype(jnp.float32)
    grad_mixed = inv_dev * (grad_in - lax.optimization_barrier(jnp.mean(grad_in, axis=-1, keepdims=True)) - normed * lax.optimization_barrier(jnp.mean(grad_in * normed, axis=-1, keepdims=True)))
    grad_low = grad_mixed.astype(jnp.bfloat16)
    proj_term = lax.dot_general(attended, grad_low, (((0,), (0,)), ((), ())), preferred_element_type=jnp.float32)
    grad_att = lax.dot_general(grad_low, proj_full, (((1,), (1,)), ((), ())), preferred_element_type=jnp.float32)
    grad_att = grad_att.astype(jnp.bfloat16).reshape(window_count, window_size, head_count, head_size)

    def backward_group(group_index):
        piece_qkv, scales = group_pieces(group_index)
        query_unit, key_unit, query_inv, key_inv, query_low, key_low, values, probability, prob_low = head_forward(piece_qkv, allowed, scales)
        grad_piece = lax.dynamic_slice_in_dim(grad_att, group_index * HEAD_GROUP, HEAD_GROUP, 2)
        grad_prob = product('wqhd,wkhd->whqk', grad_piece, values)
        grad_values = product('whqk,wqhd->wkhd', prob_low, grad_piece)
        grad_scores = probability * (grad_prob - lax.optimization_barrier(jnp.sum(probability * grad_prob, axis=-1, keepdims=True)))
        scaled_low = (grad_scores * scales[None, :, None, None]).astype(jnp.bfloat16)
        grad_qunit = product('whqk,wkhd->wqhd', scaled_low, key_low)
        grad_kunit = product('whqk,wqhd->wkhd', scaled_low, query_low)
        grad_query = query_inv * (grad_qunit - query_unit * lax.optimization_barrier(jnp.sum(grad_qunit * query_unit, axis=-1, keepdims=True)))
        grad_key = key_inv * (grad_kunit - key_unit * lax.optimization_barrier(jnp.sum(grad_kunit * key_unit, axis=-1, keepdims=True)))
        return jnp.stack([grad_query, grad_key, grad_values], axis=3).astype(jnp.bfloat16)
    grad_packed = lax.map(backward_group, group_ids)
    grad_packed = jnp.moveaxis(grad_packed, 0, 2).reshape(window_count * window_size, 3 * inner_width)
    grad_rows = lax.dot_general(grad_packed, qkv_full, (((1,), (1,)), ((), ())), preferred_element_type=jnp.float32)
    grad_rows = grad_rows.astype(jnp.bfloat16)
    return (branch.reshape(window_count, window_size, channels), grad_rows.reshape(window_count, window_size, channels), proj_term)

def reference(tokens, cotangent, region, qkv_weight, proj_weight, logit_scale):
    depth_cells, height_cells, width_cells, channels = tokens.shape
    shifted = jnp.roll(tokens, (-SD, -SH, -SW), axis=(0, 1, 2))
    shifted_grad = jnp.roll(cotangent, (-SD, -SH, -SW), axis=(0, 1, 2))
    windows_x = to_windows(shifted)
    windows_g = to_windows(shifted_grad)
    windows_region = to_windows(region)
    window_count = windows_x.shape[0]
    per_block = math.gcd(window_count, 8)
    blocks = window_count // per_block
    window_size = windows_x.shape[1]
    blocked_x = windows_x.reshape(blocks, per_block, window_size, channels)
    blocked_g = windows_g.reshape(blocks, per_block, window_size, channels)
    blocked_r = windows_region.reshape(blocks, per_block, window_size)

    def scan_step(running, pieces):
        branch, grad_rows, proj_term = window_block(pieces[0], pieces[1], pieces[2], qkv_weight, proj_weight, logit_scale)
        return (running + proj_term, (branch, grad_rows))
    zeros_start = jnp.zeros(proj_weight.shape, jnp.float32)
    proj_sum, (branches, grads) = lax.scan(scan_step, zeros_start, (blocked_x, blocked_g, blocked_r))
    branch_grid = from_windows(branches.reshape(window_count, window_size, channels), depth_cells, height_cells, width_cells)
    grad_grid = from_windows(grads.reshape(window_count, window_size, channels), depth_cells, height_cells, width_cells)
    branch_grid = jnp.roll(branch_grid, (SD, SH, SW), axis=(0, 1, 2))
    grad_grid = jnp.roll(grad_grid, (SD, SH, SW), axis=(0, 1, 2))
    block_output = (tokens.astype(jnp.float32) + branch_grid.astype(jnp.float32)).astype(jnp.bfloat16)
    token_grad = (cotangent.astype(jnp.float32) + grad_grid.astype(jnp.float32)).astype(jnp.bfloat16)
    proj_grad = proj_sum * (1.0 / math.sqrt(TOKENS))
    return (block_output, token_grad, proj_grad)
```

```python
import functools
import math

import jax
import jax.numpy as jnp
from jax import lax
from jax.experimental import pallas as pl
from jax.experimental.pallas import tpu as pltpu
from jax.sharding import PartitionSpec as P

HEAD_GROUP = 4
WD = 4
WH = 8
WW = 8
SD = 2
SH = 4
SW = 4


def shifted_2(value, axis, steps):
    count = lax.axis_size(axis)
    pairs = [(source, (source + steps) % count) for source in range(count)]
    return lax.ppermute(value, axis, pairs)


def to_windows(field):
    depth_cells, height_cells, width_cells = (field.shape[0], field.shape[1], field.shape[2])
    trailing = tuple(field.shape[3:])
    blocked = field.reshape(
        (depth_cells // WD, WD, height_cells // WH, WH, width_cells // WW, WW) + trailing
    )
    axes_order = (0, 2, 4, 1, 3, 5) + tuple(range(6, 6 + len(trailing)))
    return blocked.transpose(axes_order).reshape((-1, WD * WH * WW) + trailing)


def from_windows(windowed, depth_cells, height_cells, width_cells):
    trailing = tuple(windowed.shape[2:])
    blocked = windowed.reshape(
        (depth_cells // WD, height_cells // WH, width_cells // WW, WD, WH, WW) + trailing
    )
    axes_order = (0, 3, 1, 4, 2, 5) + tuple(range(6, 6 + len(trailing)))
    return blocked.transpose(axes_order).reshape(
        (depth_cells, height_cells, width_cells) + trailing
    )


def product(pattern, left_side, right_side):
    return jnp.einsum(pattern, left_side, right_side, preferred_element_type=jnp.float32)


def head_forward(piece_qkv, allowed, scales):
    queries = piece_qkv[:, :, :, 0].astype(jnp.float32)
    key_rows = piece_qkv[:, :, :, 1].astype(jnp.float32)
    values = piece_qkv[:, :, :, 2]
    query_inv = lax.rsqrt(jnp.sum(queries * queries, axis=-1, keepdims=True) + 1e-06)
    key_inv = lax.rsqrt(jnp.sum(key_rows * key_rows, axis=-1, keepdims=True) + 1e-06)
    query_unit = queries * query_inv
    key_unit = key_rows * key_inv
    query_low = query_unit.astype(jnp.bfloat16)
    key_low = key_unit.astype(jnp.bfloat16)
    scores = product("wqhd,wkhd->whqk", query_low, key_low) * scales[None, :, None, None]
    raised = jnp.where(allowed[:, None], jnp.exp(scores), 0.0)
    probability = raised / jnp.sum(raised, axis=-1, keepdims=True)
    prob_low = probability.astype(jnp.bfloat16)
    return (
        query_unit,
        key_unit,
        query_inv,
        key_inv,
        query_low,
        key_low,
        values,
        probability,
        prob_low,
    )


def window_block(windows_x, windows_g, windows_region, qkv_full, proj_full, logit_scale):
    window_count, window_size, channels = windows_x.shape
    head_count = logit_scale.shape[0]
    inner_width = proj_full.shape[0]
    head_size = inner_width // head_count
    group_count = head_count // HEAD_GROUP
    flat_rows = windows_x.reshape(window_count * window_size, channels)
    packed = jnp.dot(flat_rows, qkv_full, preferred_element_type=jnp.float32).astype(jnp.bfloat16)
    packed = packed.reshape(window_count, window_size, head_count, 3, head_size)
    allowed = windows_region[:, :, None] == windows_region[:, None, :]
    group_ids = jnp.arange(group_count, dtype=jnp.int32)

    def group_pieces(group_index):
        piece_qkv = lax.dynamic_slice_in_dim(packed, group_index * HEAD_GROUP, HEAD_GROUP, 2)
        scales = lax.dynamic_slice_in_dim(logit_scale, group_index * HEAD_GROUP, HEAD_GROUP, 0)
        return (piece_qkv, scales)

    def forward_group(group_index):
        piece_qkv, scales = group_pieces(group_index)
        outs_fwd = head_forward(piece_qkv, allowed, scales)
        return product("whqk,wkhd->wqhd", outs_fwd[8], outs_fwd[6]).astype(jnp.bfloat16)

    attended = lax.map(forward_group, group_ids)
    attended = jnp.moveaxis(attended, 0, 2).reshape(window_count * window_size, inner_width)
    mixed_rows = jnp.dot(attended, proj_full, preferred_element_type=jnp.float32)
    centered = mixed_rows - jnp.mean(mixed_rows, axis=-1, keepdims=True)
    inv_dev = lax.rsqrt(jnp.mean(centered * centered, axis=-1, keepdims=True) + 1e-05)
    normed = centered * inv_dev
    branch = normed.astype(jnp.bfloat16)
    grad_in = windows_g.reshape(window_count * window_size, channels).astype(jnp.float32)
    grad_mixed = inv_dev * (
        grad_in
        - jnp.mean(grad_in, axis=-1, keepdims=True)
        - normed * jnp.mean(grad_in * normed, axis=-1, keepdims=True)
    )
    grad_low = grad_mixed.astype(jnp.bfloat16)
    proj_term = lax.dot_general(
        attended, grad_low, (((0,), (0,)), ((), ())), preferred_element_type=jnp.float32
    )
    grad_att = lax.dot_general(
        grad_low, proj_full, (((1,), (1,)), ((), ())), preferred_element_type=jnp.float32
    )
    grad_att = grad_att.astype(jnp.bfloat16).reshape(
        window_count, window_size, head_count, head_size
    )

    def backward_group(group_index):
        piece_qkv, scales = group_pieces(group_index)
        (
            query_unit,
            key_unit,
            query_inv,
            key_inv,
            query_low,
            key_low,
            values,
            probability,
            prob_low,
        ) = head_forward(piece_qkv, allowed, scales)
        grad_piece = lax.dynamic_slice_in_dim(grad_att, group_index * HEAD_GROUP, HEAD_GROUP, 2)
        grad_prob = product("wqhd,wkhd->whqk", grad_piece, values)
        grad_values = product("whqk,wqhd->wkhd", prob_low, grad_piece)
        grad_scores = probability * (
            grad_prob - jnp.sum(probability * grad_prob, axis=-1, keepdims=True)
        )
        scaled_low = (grad_scores * scales[None, :, None, None]).astype(jnp.bfloat16)
        grad_qunit = product("whqk,wkhd->wqhd", scaled_low, key_low)
        grad_kunit = product("whqk,wqhd->wkhd", scaled_low, query_low)
        grad_query = query_inv * (
            grad_qunit - query_unit * jnp.sum(grad_qunit * query_unit, axis=-1, keepdims=True)
        )
        grad_key = key_inv * (
            grad_kunit - key_unit * jnp.sum(grad_kunit * key_unit, axis=-1, keepdims=True)
        )
        return jnp.stack([grad_query, grad_key, grad_values], axis=3).astype(jnp.bfloat16)

    grad_packed = lax.map(backward_group, group_ids)
    grad_packed = jnp.moveaxis(grad_packed, 0, 2).reshape(
        window_count * window_size, 3 * inner_width
    )
    grad_rows = lax.dot_general(
        grad_packed, qkv_full, (((1,), (1,)), ((), ())), preferred_element_type=jnp.float32
    )
    grad_rows = grad_rows.astype(jnp.bfloat16)
    return (
        branch.reshape(window_count, window_size, channels),
        grad_rows.reshape(window_count, window_size, channels),
        proj_term,
    )


def shards(tokens, cotangent, region, qkv_weight, proj_weight, logit_scale):
    depth_cells, height_cells, width_cells, channels = tokens.shape
    rim_pair = jnp.stack([tokens[:, :, :SW], cotangent[:, :, :SW]])
    arrived = shifted_2(rim_pair, "space", -1)
    across_tok = jnp.concatenate([tokens[:, :, SW:], arrived[0]], axis=2)
    across_grad = jnp.concatenate([cotangent[:, :, SW:], arrived[1]], axis=2)
    row_pair = jnp.stack([across_tok[:, :SH], across_grad[:, :SH]])
    arrived_rows = shifted_2(row_pair, "dp", -1)
    shifted = jnp.roll(jnp.concatenate([across_tok[:, SH:], arrived_rows[0]], axis=1), -SD, axis=0)
    shifted_grad = jnp.roll(
        jnp.concatenate([across_grad[:, SH:], arrived_rows[1]], axis=1), -SD, axis=0
    )
    qkv_full, proj_full = (
        lax.all_gather(qkv_weight, ("space", "dp"), axis=0, tiled=True),
        lax.all_gather(proj_weight, ("space", "dp"), axis=1, tiled=True),
    )
    branch_w, grad_w, proj_term = window_block(
        to_windows(shifted),
        to_windows(shifted_grad),
        to_windows(region),
        qkv_full,
        proj_full,
        logit_scale,
    )
    branch = jnp.roll(from_windows(branch_w, depth_cells, height_cells, width_cells), SD, axis=0)
    grad_grid = jnp.roll(from_windows(grad_w, depth_cells, height_cells, width_cells), SD, axis=0)
    back_rows = jnp.stack([branch[:, -SH:], grad_grid[:, -SH:]])
    came_rows = shifted_2(back_rows, "dp", 1)
    branch = jnp.concatenate([came_rows[0], branch[:, :-SH]], axis=1)
    grad_grid = jnp.concatenate([came_rows[1], grad_grid[:, :-SH]], axis=1)
    back_rims = jnp.stack([branch[:, :, -SW:], grad_grid[:, :, -SW:]])
    came_rims = shifted_2(back_rims, "space", 1)
    branch = jnp.concatenate([came_rims[0], branch[:, :, :-SW]], axis=2)
    grad_grid = jnp.concatenate([came_rims[1], grad_grid[:, :, :-SW]], axis=2)
    block_output = (tokens.astype(jnp.float32) + branch.astype(jnp.float32)).astype(jnp.bfloat16)
    token_grad = (cotangent.astype(jnp.float32) + grad_grid.astype(jnp.float32)).astype(
        jnp.bfloat16
    )
    summed = lax.psum_scatter(proj_term, ("space", "dp"), scatter_dimension=1, tiled=True)
    token_total = (
        depth_cells * height_cells * width_cells * lax.axis_size("space") * lax.axis_size("dp")
    )
    proj_grad = summed * (1.0 / math.sqrt(token_total))
    return (block_output, token_grad, proj_grad)


MESH = pl.DeviceIdType.MESH
F32 = jnp.float32
BF16 = jnp.bfloat16
PIECES = 4


def dot_nn(a, b):
    return lax.dot_general(a, b, (((1,), (0,)), ((), ())), preferred_element_type=F32)


def dot_nt(a, b):
    return lax.dot_general(a, b, (((1,), (1,)), ((), ())), preferred_element_type=F32)


def dot_tn(a, b):
    return lax.dot_general(a, b, (((0,), (0,)), ((), ())), preferred_element_type=F32)


def unit_parts(rows):
    wide = rows.astype(F32)
    inv = lax.rsqrt(jnp.sum(wide * wide, axis=-1, keepdims=True) + 1e-06)
    unit = wide * inv
    return unit, inv, unit.astype(BF16)


def slab_kernel(
    nz, heads, size, scale_out,
    scales, fields, region, own,
    out, pgrad,
    w, halo, back, packed, prob, att, gatt, gpacked, allowed_ref,
    gsend, grecv, hsend, hrecv, zsend, zrecv,
    send_sems, recv_sems,
):
    y, s, c = lax.axis_index("groups"), lax.axis_index("space"), lax.axis_index("dp")
    ns = nz * 2
    z, x = s // 2, s % 2
    chans = own.shape[-1]
    half_w = chans // 2

    def dev(yy, ss, cc):
        return {"groups": yy, "space": ss, "dp": cc}

    x_next = z * 2 + (1 - x)
    zs = [lax.rem(z + k, nz) for k in range(1, nz)]
    z_devs = [dev(y, zz * 2 + x, c) for zz in zs]
    x_dev, y_dev, core_dev = dev(y, x_next, c), dev(1 - y, s, c), dev(y, s, 1 - c)
    before, after = lax.rem(s + ns - 1, ns), lax.rem(s + 1, ns)
    barrier = pltpu.get_barrier_semaphore()
    peers = z_devs + [x_dev, y_dev, core_dev]
    peers += [dev(y, ss, cc) for ss in (before, after) for cc in (c, 1 - c)]
    for peer in peers:
        pl.semaphore_signal(barrier, inc=1, device_id=peer, device_id_type=MESH)
    pl.semaphore_wait(barrier, len(peers))

    made = []

    def copy(src, dst, where):
        index = len(made)
        made.append(
            pltpu.make_async_remote_copy(
                src_ref=src, dst_ref=dst, send_sem=send_sems.at[index],
                recv_sem=recv_sems.at[index], device_id=where, device_id_type=MESH,
            )
        )
        return made[-1]

    def lanes(which):
        return pl.ds(pl.multiple_of(which * half_w, 128), half_w)

    def goes(q):
        hi, wi = q // 2, q % 2
        return dev(y, s if wi else before, c if hi else 1 - c)

    def came(q):
        hi, wi = q // 2, q % 2
        return dev(y, s if wi else after, c if hi else 1 - c)

    halos = [[copy(fields.at[f, q], halo.at[f, q], goes(q)) for q in range(3)] for f in range(2)]
    mine, other = lanes(y), lanes(1 - y)
    first_y = c == 0
    s_a, y_a = jnp.where(first_y, s, x_next), jnp.where(first_y, 1 - y, y)
    s_b, y_b = jnp.where(first_y, x_next, s), jnp.where(first_y, y, 1 - y)
    a_dev, b_dev = dev(y_a, s_a, c), dev(y_b, s_b, c)
    x_a = jnp.where(first_y, x, 1 - x)
    got_a = lanes(y_a)
    st1 = [
        [copy(own.at[p, :, mine], w.at[p, z, x, c, :, mine], zd) for zd in z_devs]
        for p in range(PIECES)
    ]
    st2, st3a, st3b, st4 = [], [], [], []
    for p in range(PIECES):
        quarter = w.at[p, :, x, c, :, mine]
        st2.append(copy(quarter, quarter, a_dev))
        st3a.append(copy(quarter, quarter, b_dev))
        second = w.at[p, :, x_a, c, :, got_a]
        st3b.append(copy(second, second, b_dev))
        whole = w.at[p, :, :, c]
        st4.append(copy(whole, whole, core_dev))

    def step1(p):
        for item in st1[p]:
            item.wait_recv()
        st2[p].start()
        st3a[p].start()

    def step2(p):
        st2[p].wait_recv()
        st3b[p].start()

    def step3(p):
        st3a[p].wait_recv()
        st3b[p].wait_recv()
        st4[p].start()

    for item in halos[0]:
        item.start()
    for p in range(PIECES):
        for item in st1[p]:
            item.start()
        if p == 1:
            for item in halos[1]:
                item.start()
    for p in range(PIECES):
        w[p, z, x, c, :, mine] = own[p, :, mine]
    labels = jnp.broadcast_to(region[...], (region.shape[1], region.shape[1]))
    allowed_ref[...] = jnp.where(labels == labels.T, 1.0, 0.0)

    step1(0)
    step1(1)
    step2(0)
    step1(2)
    step2(1)
    step3(0)
    step1(3)
    step2(2)
    step3(1)

    def window(f):
        for item in halos[f]:
            item.wait_recv()
        return jnp.concatenate([halo[f, 0], halo[f, 1], halo[f, 2], fields[f, 3]], axis=0)

    per_piece = heads // 3
    pairs = per_piece // 2

    def weight(p):
        return w[p].reshape(-1, chans)

    def forward(p, rows):
        st4[p].wait_recv()
        packed[p] = dot_nn(rows, weight(p)).astype(BF16)

        @pl.loop(0, pairs)
        def _(pair):
            piece = packed[p, :, pl.ds(pl.multiple_of(pair * 6 * size, 128), 6 * size)]
            outs = []
            for i in range(2):
                head = p * per_piece + pair * 2 + i
                q, k, v = [piece[:, (3 * i + j) * size:(3 * i + j + 1) * size] for j in range(3)]
                q_low, k_low = unit_parts(q)[2], unit_parts(k)[2]
                scores = dot_nt(q_low, k_low) * scales[head]
                raised = jnp.exp(scores) * allowed_ref[...]
                probability = raised / jnp.sum(raised, axis=-1, keepdims=True)
                prob[head] = probability
                outs.append(dot_nn(probability.astype(BF16), v).astype(BF16))
            at = p * per_piece * size + pair * 2 * size
            att[:, pl.ds(pl.multiple_of(at, 128), 2 * size)] = jnp.concatenate(outs, axis=1)

    rows = window(0)
    forward(0, rows)
    step2(3)
    step3(2)
    forward(1, rows)
    step3(3)
    forward(2, rows)
    st4[3].wait_recv()

    attended = att[...]
    mixed = dot_nt(attended, weight(3))
    centered = mixed - jnp.mean(mixed, axis=-1, keepdims=True)
    inv_dev = lax.rsqrt(jnp.mean(centered * centered, axis=-1, keepdims=True) + 1e-05)
    normed = centered * inv_dev
    result = (rows.astype(F32) + normed.astype(BF16).astype(F32)).astype(BF16)
    quad = out.shape[2]
    returns = [[copy(back.at[f, q], out.at[f, q], came(q)) for q in range(3)] for f in range(2)]
    for q in range(3):
        back[0, q] = result[q * quad:(q + 1) * quad]
        returns[0][q].start()
    out[0, 3] = result[3 * quad:]
    grad_in = window(1).astype(F32)
    grad_low = (
        inv_dev
        * (
            grad_in
            - jnp.mean(grad_in, axis=-1, keepdims=True)
            - normed * jnp.mean(grad_in * normed, axis=-1, keepdims=True)
        )
    ).astype(BF16)
    gsend[...] = dot_tn(grad_low, attended).astype(BF16).reshape(gsend.shape)
    to_core = copy(gsend.at[:, :, 1 - c], grecv, core_dev)
    to_core.start()
    gatt[...] = dot_nn(grad_low, weight(3)).astype(BF16)

    def backward(p):
        @pl.loop(0, pairs)
        def _(pair):
            at = pl.ds(pl.multiple_of(pair * 6 * size, 128), 6 * size)
            piece = packed[p, :, at]
            g_at = p * per_piece * size + pair * 2 * size
            g_pair = gatt[:, pl.ds(pl.multiple_of(g_at, 128), 2 * size)]
            outs = []
            for i in range(2):
                head = p * per_piece + pair * 2 + i
                q, k, v = [piece[:, (3 * i + j) * size:(3 * i + j + 1) * size] for j in range(3)]
                q_unit, q_inv, q_low = unit_parts(q)
                k_unit, k_inv, k_low = unit_parts(k)
                g = g_pair[:, i * size:(i + 1) * size]
                probability = prob[head]
                g_prob = dot_nt(g, v)
                g_val = dot_tn(probability.astype(BF16), g)
                inner = jnp.sum(probability * g_prob, axis=-1, keepdims=True)
                scaled = (probability * (g_prob - inner) * scales[head]).astype(BF16)
                g_q = dot_nn(scaled, k_low)
                g_k = dot_tn(scaled, q_low)
                g_q = q_inv * (g_q - q_unit * jnp.sum(g_q * q_unit, axis=-1, keepdims=True))
                g_k = k_inv * (g_k - k_unit * jnp.sum(g_k * k_unit, axis=-1, keepdims=True))
                outs += [g_q.astype(BF16), g_k.astype(BF16), g_val.astype(BF16)]
            gpacked[p, :, at] = jnp.concatenate(outs, axis=1)

    backward(0)
    to_core.wait_recv()
    hsend[...] = (gsend[:, :, c].astype(F32) + grecv[...].astype(F32)).astype(BF16)
    to_x = copy(hsend.at[:, 1 - x], hrecv, x_dev)
    to_x.start()
    backward(1)
    to_x.wait_recv()
    zsend[...] = (hsend[:, x].astype(F32) + hrecv[...].astype(F32)).astype(BF16)
    to_z = [copy(zsend.at[zz], zrecv.at[k], zd) for k, (zz, zd) in enumerate(zip(zs, z_devs))]
    for item in to_z:
        item.start()
    backward(2)
    grad_rows = dot_nt(gpacked[0], weight(0))
    grad_rows += dot_nt(gpacked[1], weight(1))
    grad_rows += dot_nt(gpacked[2], weight(2))
    grad_out = (grad_in + grad_rows.astype(BF16).astype(F32)).astype(BF16)
    for q in range(3):
        back[1, q] = grad_out[q * quad:(q + 1) * quad]
        returns[1][q].start()
    out[1, 3] = grad_out[3 * quad:]
    total = zsend[z].astype(F32)
    for k, item in enumerate(to_z):
        item.wait_recv()
        total += zrecv[k].astype(F32)
    pgrad[...] = total * scale_out
    for item in returns[0] + returns[1]:
        item.wait_recv()
    for item in made:
        item.wait_send()


def to_quads(field):
    lead = field.shape[0]
    rest = tuple(field.shape[4:])
    d, h, wd = field.shape[1:4]
    split = field.reshape((lead, d, 2, h // 2, 2, wd // 2) + rest)
    order = (0, 2, 4, 1, 3, 5) + tuple(range(6, 6 + len(rest)))
    return split.transpose(order).reshape((lead, 4, d * h * wd // 4) + rest)


def from_quads(quads, d, h, wd):
    lead, chans = quads.shape[0], quads.shape[-1]
    split = quads.reshape(lead, 2, 2, d, h // 2, wd // 2, chans)
    return split.transpose(0, 3, 1, 4, 2, 5, 6).reshape(lead, d, h, wd, chans)


def fused_shards(tokens, cotangent, region, qkv_weight, proj_weight, logit_scale):
    d, h, wd, chans = tokens.shape
    heads = logit_scale.shape[0]
    space = lax.axis_size("space")
    nz = space // 2
    count = d * h * wd
    share = qkv_weight.shape[0]
    fields = to_quads(jnp.stack([tokens, cotangent]))
    labels = to_quads(jnp.roll(region, (SD, SH, SW), axis=(0, 1, 2))[None])
    labels = labels.astype(F32).reshape(1, count)
    own = jnp.concatenate(
        [qkv_weight.reshape(share, 3, chans).transpose(1, 0, 2), proj_weight.T[None]], axis=0
    )
    copies = 6 + PIECES * (nz - 1) + 4 * PIECES + 6 + 2 + nz - 1
    vmem = pl.BlockSpec(memory_space=pltpu.VMEM)
    scale_out = 1.0 / math.sqrt(count * space * lax.axis_size("dp"))
    out, pgrad = pl.pallas_call(
        functools.partial(slab_kernel, nz, heads, chans // heads, scale_out),
        out_shape=[
            jax.ShapeDtypeStruct(fields.shape, BF16),
            jax.ShapeDtypeStruct((share, chans), F32),
        ],
        in_specs=[pl.BlockSpec(memory_space=pltpu.SMEM), vmem, vmem, vmem],
        out_specs=[vmem, vmem],
        scratch_shapes=[
            pltpu.VMEM((PIECES, nz, 2, 2, share, chans), BF16),
            pltpu.VMEM((2, 3, count // 4, chans), BF16),
            pltpu.VMEM((2, 3, count // 4, chans), BF16),
            pltpu.VMEM((3, count, chans), BF16),
            pltpu.VMEM((heads, count, count), F32),
            pltpu.VMEM((count, chans), BF16),
            pltpu.VMEM((count, chans), BF16),
            pltpu.VMEM((3, count, chans), BF16),
            pltpu.VMEM((count, count), F32),
            pltpu.VMEM((nz, 2, 2, share, chans), BF16),
            pltpu.VMEM((nz, 2, share, chans), BF16),
            pltpu.VMEM((nz, 2, share, chans), BF16),
            pltpu.VMEM((nz, share, chans), BF16),
            pltpu.VMEM((nz, share, chans), BF16),
            pltpu.VMEM((nz - 1, share, chans), BF16),
            pltpu.SemaphoreType.DMA((copies,)),
            pltpu.SemaphoreType.DMA((copies,)),
        ],
        compiler_params=pltpu.CompilerParams(
            collective_id=0, has_side_effects=True, vmem_limit_bytes=48 * 1024 * 1024
        ),
    )(logit_scale, fields, labels, own)
    grids = from_quads(out, d, h, wd)
    return (grids[0], grids[1], pgrad.T)


def block(tokens, cotangent, region, qkv_weight, proj_weight, logit_scale):
    sizes = [lax.axis_size(axis) for axis in ("groups", "space", "dp")]
    share = qkv_weight.shape[0]
    fits = sizes[0] == 2 and sizes[2] == 2 and sizes[1] % 2 == 0 and sizes[1] >= 4
    body = fused_shards if fits and share % 16 == 0 and tokens.shape[0] == WD else shards
    return body(tokens, cotangent, region, qkv_weight, proj_weight, logit_scale)


def solution(mesh):
    in_specs = (
        P("groups", "dp", "space", None),
        P("groups", "dp", "space", None),
        P("groups", "dp", "space"),
        P(("space", "dp"), None),
        P(None, ("space", "dp")),
        P(),
    )
    out_specs = (
        P("groups", "dp", "space", None),
        P("groups", "dp", "space", None),
        P("groups", ("space", "dp")),
    )
    return jax.shard_map(
        block, mesh=mesh, in_specs=in_specs, out_specs=out_specs, check_vma=False
    )
```

```python
import functools
import math

import jax
import jax.numpy as jnp
from jax import lax
from jax.experimental import pallas as pl
from jax.experimental.pallas import tpu as pltpu
from jax.sharding import PartitionSpec as P

HEAD_GROUP = 4
WD = 4
WH = 8
WW = 8
SD = 2
SH = 4
SW = 4


def shifted_2(value, axis, steps):
    count = lax.axis_size(axis)
    pairs = [(source, (source + steps) % count) for source in range(count)]
    return lax.ppermute(value, axis, pairs)


def to_windows(field):
    depth_cells, height_cells, width_cells = (field.shape[0], field.shape[1], field.shape[2])
    trailing = tuple(field.shape[3:])
    blocked = field.reshape(
        (depth_cells // WD, WD, height_cells // WH, WH, width_cells // WW, WW) + trailing
    )
    axes_order = (0, 2, 4, 1, 3, 5) + tuple(range(6, 6 + len(trailing)))
    return blocked.transpose(axes_order).reshape((-1, WD * WH * WW) + trailing)


def from_windows(windowed, depth_cells, height_cells, width_cells):
    trailing = tuple(windowed.shape[2:])
    blocked = windowed.reshape(
        (depth_cells // WD, height_cells // WH, width_cells // WW, WD, WH, WW) + trailing
    )
    axes_order = (0, 3, 1, 4, 2, 5) + tuple(range(6, 6 + len(trailing)))
    return blocked.transpose(axes_order).reshape(
        (depth_cells, height_cells, width_cells) + trailing
    )


def product(pattern, left_side, right_side):
    return jnp.einsum(pattern, left_side, right_side, preferred_element_type=jnp.float32)


def head_forward(piece_qkv, allowed, scales):
    queries = piece_qkv[:, :, :, 0].astype(jnp.float32)
    key_rows = piece_qkv[:, :, :, 1].astype(jnp.float32)
    values = piece_qkv[:, :, :, 2]
    query_inv = lax.rsqrt(jnp.sum(queries * queries, axis=-1, keepdims=True) + 1e-06)
    key_inv = lax.rsqrt(jnp.sum(key_rows * key_rows, axis=-1, keepdims=True) + 1e-06)
    query_unit = queries * query_inv
    key_unit = key_rows * key_inv
    query_low = query_unit.astype(jnp.bfloat16)
    key_low = key_unit.astype(jnp.bfloat16)
    scores = product("wqhd,wkhd->whqk", query_low, key_low) * scales[None, :, None, None]
    raised = jnp.where(allowed[:, None], jnp.exp(scores), 0.0)
    probability = raised / jnp.sum(raised, axis=-1, keepdims=True)
    prob_low = probability.astype(jnp.bfloat16)
    return (
        query_unit,
        key_unit,
        query_inv,
        key_inv,
        query_low,
        key_low,
        values,
        probability,
        prob_low,
    )


def window_block(windows_x, windows_g, windows_region, qkv_full, proj_full, logit_scale):
    window_count, window_size, channels = windows_x.shape
    head_count = logit_scale.shape[0]
    inner_width = proj_full.shape[0]
    head_size = inner_width // head_count
    group_count = head_count // HEAD_GROUP
    flat_rows = windows_x.reshape(window_count * window_size, channels)
    packed = jnp.dot(flat_rows, qkv_full, preferred_element_type=jnp.float32).astype(jnp.bfloat16)
    packed = packed.reshape(window_count, window_size, head_count, 3, head_size)
    allowed = windows_region[:, :, None] == windows_region[:, None, :]
    group_ids = jnp.arange(group_count, dtype=jnp.int32)

    def group_pieces(group_index):
        piece_qkv = lax.dynamic_slice_in_dim(packed, group_index * HEAD_GROUP, HEAD_GROUP, 2)
        scales = lax.dynamic_slice_in_dim(logit_scale, group_index * HEAD_GROUP, HEAD_GROUP, 0)
        return (piece_qkv, scales)

    def forward_group(group_index):
        piece_qkv, scales = group_pieces(group_index)
        outs_fwd = head_forward(piece_qkv, allowed, scales)
        return product("whqk,wkhd->wqhd", outs_fwd[8], outs_fwd[6]).astype(jnp.bfloat16)

    attended = lax.map(forward_group, group_ids)
    attended = jnp.moveaxis(attended, 0, 2).reshape(window_count * window_size, inner_width)
    mixed_rows = jnp.dot(attended, proj_full, preferred_element_type=jnp.float32)
    centered = mixed_rows - jnp.mean(mixed_rows, axis=-1, keepdims=True)
    inv_dev = lax.rsqrt(jnp.mean(centered * centered, axis=-1, keepdims=True) + 1e-05)
    normed = centered * inv_dev
    branch = normed.astype(jnp.bfloat16)
    grad_in = windows_g.reshape(window_count * window_size, channels).astype(jnp.float32)
    grad_mixed = inv_dev * (
        grad_in
        - jnp.mean(grad_in, axis=-1, keepdims=True)
        - normed * jnp.mean(grad_in * normed, axis=-1, keepdims=True)
    )
    grad_low = grad_mixed.astype(jnp.bfloat16)
    proj_term = lax.dot_general(
        attended, grad_low, (((0,), (0,)), ((), ())), preferred_element_type=jnp.float32
    )
    grad_att = lax.dot_general(
        grad_low, proj_full, (((1,), (1,)), ((), ())), preferred_element_type=jnp.float32
    )
    grad_att = grad_att.astype(jnp.bfloat16).reshape(
        window_count, window_size, head_count, head_size
    )

    def backward_group(group_index):
        piece_qkv, scales = group_pieces(group_index)
        (
            query_unit,
            key_unit,
            query_inv,
            key_inv,
            query_low,
            key_low,
            values,
            probability,
            prob_low,
        ) = head_forward(piece_qkv, allowed, scales)
        grad_piece = lax.dynamic_slice_in_dim(grad_att, group_index * HEAD_GROUP, HEAD_GROUP, 2)
        grad_prob = product("wqhd,wkhd->whqk", grad_piece, values)
        grad_values = product("whqk,wqhd->wkhd", prob_low, grad_piece)
        grad_scores = probability * (
            grad_prob - jnp.sum(probability * grad_prob, axis=-1, keepdims=True)
        )
        scaled_low = (grad_scores * scales[None, :, None, None]).astype(jnp.bfloat16)
        grad_qunit = product("whqk,wkhd->wqhd", scaled_low, key_low)
        grad_kunit = product("whqk,wqhd->wkhd", scaled_low, query_low)
        grad_query = query_inv * (
            grad_qunit - query_unit * jnp.sum(grad_qunit * query_unit, axis=-1, keepdims=True)
        )
        grad_key = key_inv * (
            grad_kunit - key_unit * jnp.sum(grad_kunit * key_unit, axis=-1, keepdims=True)
        )
        return jnp.stack([grad_query, grad_key, grad_values], axis=3).astype(jnp.bfloat16)

    grad_packed = lax.map(backward_group, group_ids)
    grad_packed = jnp.moveaxis(grad_packed, 0, 2).reshape(
        window_count * window_size, 3 * inner_width
    )
    grad_rows = lax.dot_general(
        grad_packed, qkv_full, (((1,), (1,)), ((), ())), preferred_element_type=jnp.float32
    )
    grad_rows = grad_rows.astype(jnp.bfloat16)
    return (
        branch.reshape(window_count, window_size, channels),
        grad_rows.reshape(window_count, window_size, channels),
        proj_term,
    )


def shards(tokens, cotangent, region, qkv_weight, proj_weight, logit_scale):
    depth_cells, height_cells, width_cells, channels = tokens.shape
    rim_pair = jnp.stack([tokens[:, :, :SW], cotangent[:, :, :SW]])
    arrived = shifted_2(rim_pair, "space", -1)
    across_tok = jnp.concatenate([tokens[:, :, SW:], arrived[0]], axis=2)
    across_grad = jnp.concatenate([cotangent[:, :, SW:], arrived[1]], axis=2)
    row_pair = jnp.stack([across_tok[:, :SH], across_grad[:, :SH]])
    arrived_rows = shifted_2(row_pair, "dp", -1)
    shifted = jnp.roll(jnp.concatenate([across_tok[:, SH:], arrived_rows[0]], axis=1), -SD, axis=0)
    shifted_grad = jnp.roll(
        jnp.concatenate([across_grad[:, SH:], arrived_rows[1]], axis=1), -SD, axis=0
    )
    qkv_full, proj_full = (
        lax.all_gather(qkv_weight, ("space", "dp"), axis=0, tiled=True),
        lax.all_gather(proj_weight, ("space", "dp"), axis=1, tiled=True),
    )
    branch_w, grad_w, proj_term = window_block(
        to_windows(shifted),
        to_windows(shifted_grad),
        to_windows(region),
        qkv_full,
        proj_full,
        logit_scale,
    )
    branch = jnp.roll(from_windows(branch_w, depth_cells, height_cells, width_cells), SD, axis=0)
    grad_grid = jnp.roll(from_windows(grad_w, depth_cells, height_cells, width_cells), SD, axis=0)
    back_rows = jnp.stack([branch[:, -SH:], grad_grid[:, -SH:]])
    came_rows = shifted_2(back_rows, "dp", 1)
    branch = jnp.concatenate([came_rows[0], branch[:, :-SH]], axis=1)
    grad_grid = jnp.concatenate([came_rows[1], grad_grid[:, :-SH]], axis=1)
    back_rims = jnp.stack([branch[:, :, -SW:], grad_grid[:, :, -SW:]])
    came_rims = shifted_2(back_rims, "space", 1)
    branch = jnp.concatenate([came_rims[0], branch[:, :, :-SW]], axis=2)
    grad_grid = jnp.concatenate([came_rims[1], grad_grid[:, :, :-SW]], axis=2)
    block_output = (tokens.astype(jnp.float32) + branch.astype(jnp.float32)).astype(jnp.bfloat16)
    token_grad = (cotangent.astype(jnp.float32) + grad_grid.astype(jnp.float32)).astype(
        jnp.bfloat16
    )
    summed = lax.psum_scatter(proj_term, ("space", "dp"), scatter_dimension=1, tiled=True)
    token_total = (
        depth_cells * height_cells * width_cells * lax.axis_size("space") * lax.axis_size("dp")
    )
    proj_grad = summed * (1.0 / math.sqrt(token_total))
    return (block_output, token_grad, proj_grad)


MESH = pl.DeviceIdType.MESH
F32 = jnp.float32
BF16 = jnp.bfloat16
PIECES = 4
LOG2E = math.log2(math.e)


def dot_nn(a, b):
    return lax.dot_general(a, b, (((1,), (0,)), ((), ())), preferred_element_type=F32)


def dot_nt(a, b):
    return lax.dot_general(a, b, (((1,), (1,)), ((), ())), preferred_element_type=F32)


def dot_tn(a, b):
    return lax.dot_general(a, b, (((0,), (0,)), ((), ())), preferred_element_type=F32)


def unit_parts(rows):
    wide = rows.astype(F32)
    inv = lax.rsqrt(jnp.sum(wide * wide, axis=-1, keepdims=True) + 1e-06)
    unit = wide * inv
    return unit, inv, unit.astype(BF16)


def slab_kernel(
    nz, heads, size, scale_out,
    scales, fields, region, own,
    out, pgrad,
    w, halo, back, packed, prob, att, gatt, gpacked, allowed_ref,
    gsend, grecv, hsend, hrecv, zsend, zrecv,
    send_sems, recv_sems,
):
    y, s, c = lax.axis_index("groups"), lax.axis_index("space"), lax.axis_index("dp")
    ns = nz * 2
    z, x = s // 2, s % 2
    chans = own.shape[-1]
    half_w = chans // 2

    def dev(yy, ss, cc):
        return {"groups": yy, "space": ss, "dp": cc}

    x_next = z * 2 + (1 - x)
    zs = [lax.rem(z + k, nz) for k in range(1, nz)]
    z_devs = [dev(y, zz * 2 + x, c) for zz in zs]
    x_dev, y_dev, core_dev = dev(y, x_next, c), dev(1 - y, s, c), dev(y, s, 1 - c)
    before, after = lax.rem(s + ns - 1, ns), lax.rem(s + 1, ns)
    barrier = pltpu.get_barrier_semaphore()
    peers = z_devs + [x_dev, y_dev, core_dev]
    peers += [dev(y, ss, cc) for ss in (before, after) for cc in (c, 1 - c)]
    for peer in peers:
        pl.semaphore_signal(barrier, inc=1, device_id=peer, device_id_type=MESH)
    pl.semaphore_wait(barrier, len(peers))

    made = []

    def copy(src, dst, where):
        index = len(made)
        made.append(
            pltpu.make_async_remote_copy(
                src_ref=src, dst_ref=dst, send_sem=send_sems.at[index],
                recv_sem=recv_sems.at[index], device_id=where, device_id_type=MESH,
            )
        )
        return made[-1]

    def lanes(which):
        return pl.ds(pl.multiple_of(which * half_w, 128), half_w)

    def goes(q):
        hi, wi = q // 2, q % 2
        return dev(y, s if wi else before, c if hi else 1 - c)

    def came(q):
        hi, wi = q // 2, q % 2
        return dev(y, s if wi else after, c if hi else 1 - c)

    halos = [[copy(fields.at[f, q], halo.at[f, q], goes(q)) for q in range(3)] for f in range(2)]
    mine = lanes(y)
    froms = [z] + [lax.rem(z + nz - k, nz) for k in range(1, nz)]
    st1, st2, st3, st3d, st4 = [], [], [], [], []
    for p in range(PIECES):
        st1.append([copy(own.at[p, :, mine], w.at[p, z, x, c, :, mine], zd) for zd in z_devs])
        quarters = [w.at[p, zf, x, c, :, mine] for zf in froms]
        st2.append([copy(own.at[p, :, mine], quarters[0], x_dev)])
        st2[p] += [copy(quarter, quarter, x_dev) for quarter in quarters[1:]]
        st3.append([copy(quarter, quarter, y_dev) for quarter in quarters[1:]])
        diagonal = [w.at[p, zf, 1 - x, c, :, mine] for zf in froms]
        st3d.append([copy(quarter, quarter, y_dev) for quarter in diagonal])
        whole = w.at[p, :, :, c]
        st4.append(copy(whole, whole, core_dev))

    def step1(p):
        for k in range(1, nz):
            st1[p][k - 1].wait_recv()
            st2[p][k].start()
            st3[p][k - 1].start()

    def step2(p):
        for arriving, onward in zip(st2[p], st3d[p]):
            arriving.wait_recv()
            onward.start()

    def step3(p):
        for item in st3[p] + st3d[p]:
            item.wait_recv()
        st4[p].start()

    for item in halos[0]:
        item.start()
    for p in range(PIECES):
        for item in [st2[p][0]] + st1[p]:
            item.start()
    for p in range(PIECES):
        w[p, z, x, c] = own[p]
    labels = jnp.broadcast_to(region[...], (region.shape[1], region.shape[1]))
    allowed_ref[...] = jnp.where(labels == labels.T, 1.0, 0.0)

    step1(0)
    step1(1)
    step2(0)
    step1(2)
    step2(1)
    step3(0)
    step1(3)
    for item in halos[1]:
        item.start()

    def window(f):
        for item in halos[f]:
            item.wait_recv()
        return jnp.concatenate([halo[f, 0], halo[f, 1], halo[f, 2], fields[f, 3]], axis=0)

    per_piece = heads // 3
    pairs = per_piece // 2

    def weight(p):
        return w[p].reshape(-1, chans)

    def forward(p, rows, between):
        st4[p].wait_recv()
        packed[p] = dot_nn(rows, weight(p)).astype(BF16)

        for pair in range(pairs):
            if pair == pairs // 2:
                between()
            piece = packed[p, :, pair * 6 * size:(pair + 1) * 6 * size]
            outs = []
            for i in range(2):
                head = p * per_piece + pair * 2 + i
                q, k, v = [piece[:, (3 * i + j) * size:(3 * i + j + 1) * size] for j in range(3)]
                q_low, k_low = unit_parts(q)[2], unit_parts(k)[2]
                scores = dot_nt(q_low, k_low) * (scales[head] * LOG2E)
                raised = jnp.exp2(scores) * allowed_ref[...]
                probability = raised * (1.0 / jnp.sum(raised, axis=-1, keepdims=True))
                prob[head] = probability
                outs.append(dot_nn(probability.astype(BF16), v).astype(BF16))
            at = p * per_piece * size + pair * 2 * size
            att[:, at:at + 2 * size] = jnp.concatenate(outs, axis=1)

    rows = window(0)
    forward(0, rows, lambda: step2(2))
    step3(1)
    forward(1, rows, lambda: step2(3))
    step3(2)
    forward(2, rows, lambda: step3(3))
    st4[3].wait_recv()

    attended = att[...]
    mixed = dot_nt(attended, weight(3))
    centered = mixed - jnp.mean(mixed, axis=-1, keepdims=True)
    inv_dev = lax.rsqrt(jnp.mean(centered * centered, axis=-1, keepdims=True) + 1e-05)
    normed = centered * inv_dev
    result = (rows.astype(F32) + normed.astype(BF16).astype(F32)).astype(BF16)
    quad = out.shape[2]
    returns = [[copy(back.at[f, q], out.at[f, q], came(q)) for q in range(3)] for f in range(2)]
    for q in (0, 2, 1):
        back[0, q] = result[q * quad:(q + 1) * quad]
        returns[0][q].start()
    out[0, 3] = result[3 * quad:]
    grad_in = window(1).astype(F32)
    grad_low = (
        inv_dev
        * (
            grad_in
            - jnp.mean(grad_in, axis=-1, keepdims=True)
            - normed * jnp.mean(grad_in * normed, axis=-1, keepdims=True)
        )
    ).astype(BF16)
    gsend[...] = dot_tn(grad_low, attended).astype(BF16).reshape(gsend.shape)
    to_core = copy(gsend.at[:, :, 1 - c], grecv, core_dev)
    to_core.start()
    gatt[...] = dot_nn(grad_low, weight(3)).astype(BF16)

    def backward(p, between):
        for pair in range(pairs):
            if pair == pairs // 2:
                between()
            at = slice(pair * 6 * size, (pair + 1) * 6 * size)
            piece = packed[p, :, at]
            g_at = p * per_piece * size + pair * 2 * size
            g_pair = gatt[:, g_at:g_at + 2 * size]
            outs = []
            for i in range(2):
                head = p * per_piece + pair * 2 + i
                q, k, v = [piece[:, (3 * i + j) * size:(3 * i + j + 1) * size] for j in range(3)]
                q_unit, q_inv, q_low = unit_parts(q)
                k_unit, k_inv, k_low = unit_parts(k)
                g = g_pair[:, i * size:(i + 1) * size]
                probability = prob[head]
                g_prob = dot_nt(g, v)
                g_val = dot_tn(probability.astype(BF16), g)
                inner = jnp.sum(probability * g_prob, axis=-1, keepdims=True)
                scaled = (probability * (g_prob - inner) * scales[head]).astype(BF16)
                g_q = dot_nn(scaled, k_low)
                g_k = dot_tn(scaled, q_low)
                g_q = q_inv * (g_q - q_unit * jnp.sum(g_q * q_unit, axis=-1, keepdims=True))
                g_k = k_inv * (g_k - k_unit * jnp.sum(g_k * k_unit, axis=-1, keepdims=True))
                outs += [g_q.astype(BF16), g_k.astype(BF16), g_val.astype(BF16)]
            gpacked[p, :, at] = jnp.concatenate(outs, axis=1)

    to_x = copy(hsend.at[:, 1 - x], hrecv, x_dev)
    to_z = [copy(zsend.at[zz], zrecv.at[k], zd) for k, (zz, zd) in enumerate(zip(zs, z_devs))]

    def to_strips():
        to_core.wait_recv()
        hsend[...] = (gsend[:, :, c].astype(F32) + grecv[...].astype(F32)).astype(BF16)
        to_x.start()

    def to_levels():
        to_x.wait_recv()
        zsend[...] = (hsend[:, x].astype(F32) + hrecv[...].astype(F32)).astype(BF16)
        for item in to_z:
            item.start()

    backward(0, to_strips)
    backward(1, lambda: None)
    backward(2, to_levels)

    def grads_of(first, second):
        total = 0.0
        for p in range(3):
            lhs = [gpacked[p, q * quad:(q + 1) * quad] for q in (first, second)]
            total += dot_nt(jnp.concatenate(lhs, axis=0), weight(p))
        for i, q in enumerate((first, second)):
            added = total[i * quad:(i + 1) * quad].astype(BF16).astype(F32)
            value = (grad_in[q * quad:(q + 1) * quad] + added).astype(BF16)
            if q < 3:
                back[1, q] = value
                returns[1][q].start()
            else:
                out[1, q] = value

    grads_of(0, 2)
    grads_of(1, 3)
    total = zsend[z].astype(F32)
    for k, item in enumerate(to_z):
        item.wait_recv()
        total += zrecv[k].astype(F32)
    pgrad[...] = total * scale_out
    for item in returns[0] + returns[1]:
        item.wait_recv()
    for item in made:
        item.wait_send()


def to_quads(field):
    lead = field.shape[0]
    rest = tuple(field.shape[4:])
    d, h, wd = field.shape[1:4]
    split = field.reshape((lead, d, 2, h // 2, 2, wd // 2) + rest)
    order = (0, 2, 4, 1, 3, 5) + tuple(range(6, 6 + len(rest)))
    return split.transpose(order).reshape((lead, 4, d * h * wd // 4) + rest)


def from_quads(quads, d, h, wd):
    lead, chans = quads.shape[0], quads.shape[-1]
    split = quads.reshape(lead, 2, 2, d, h // 2, wd // 2, chans)
    return split.transpose(0, 3, 1, 4, 2, 5, 6).reshape(lead, d, h, wd, chans)


def fused_shards(tokens, cotangent, region, qkv_weight, proj_weight, logit_scale):
    d, h, wd, chans = tokens.shape
    heads = logit_scale.shape[0]
    space = lax.axis_size("space")
    nz = space // 2
    count = d * h * wd
    share = qkv_weight.shape[0]
    fields = to_quads(jnp.stack([tokens, cotangent]))
    labels = to_quads(jnp.roll(region, (SD, SH, SW), axis=(0, 1, 2))[None])
    labels = labels.astype(F32).reshape(1, count)
    own = jnp.concatenate(
        [qkv_weight.reshape(share, 3, chans).transpose(1, 0, 2), proj_weight.T[None]], axis=0
    )
    copies = 6 + PIECES * (2 * (nz - 1) + 2 * nz + 1) + 6 + 2 + nz - 1
    vmem = pl.BlockSpec(memory_space=pltpu.VMEM)
    scale_out = 1.0 / math.sqrt(count * space * lax.axis_size("dp"))
    out, pgrad = pl.pallas_call(
        functools.partial(slab_kernel, nz, heads, chans // heads, scale_out),
        out_shape=[
            jax.ShapeDtypeStruct(fields.shape, BF16),
            jax.ShapeDtypeStruct((share, chans), F32),
        ],
        in_specs=[pl.BlockSpec(memory_space=pltpu.SMEM), vmem, vmem, vmem],
        out_specs=[vmem, vmem],
        scratch_shapes=[
            pltpu.VMEM((PIECES, nz, 2, 2, share, chans), BF16),
            pltpu.VMEM((2, 3, count // 4, chans), BF16),
            pltpu.VMEM((2, 3, count // 4, chans), BF16),
            pltpu.VMEM((3, count, chans), BF16),
            pltpu.VMEM((heads, count, count), F32),
            pltpu.VMEM((count, chans), BF16),
            pltpu.VMEM((count, chans), BF16),
            pltpu.VMEM((3, count, chans), BF16),
            pltpu.VMEM((count, count), F32),
            pltpu.VMEM((nz, 2, 2, share, chans), BF16),
            pltpu.VMEM((nz, 2, share, chans), BF16),
            pltpu.VMEM((nz, 2, share, chans), BF16),
            pltpu.VMEM((nz, share, chans), BF16),
            pltpu.VMEM((nz, share, chans), BF16),
            pltpu.VMEM((nz - 1, share, chans), BF16),
            pltpu.SemaphoreType.DMA((copies,)),
            pltpu.SemaphoreType.DMA((copies,)),
        ],
        compiler_params=pltpu.CompilerParams(
            collective_id=0, has_side_effects=True, vmem_limit_bytes=48 * 1024 * 1024
        ),
    )(logit_scale, fields, labels, own)
    grids = from_quads(out, d, h, wd)
    return (grids[0], grids[1], pgrad.T)


def block(tokens, cotangent, region, qkv_weight, proj_weight, logit_scale):
    sizes = [lax.axis_size(axis) for axis in ("groups", "space", "dp")]
    share = qkv_weight.shape[0]
    fits = sizes[0] == 2 and sizes[2] == 2 and sizes[1] % 2 == 0 and sizes[1] >= 4
    body = fused_shards if fits and share % 16 == 0 and tokens.shape[0] == WD else shards
    return body(tokens, cotangent, region, qkv_weight, proj_weight, logit_scale)


def solution(mesh):
    in_specs = (
        P("groups", "dp", "space", None),
        P("groups", "dp", "space", None),
        P("groups", "dp", "space"),
        P(("space", "dp"), None),
        P(None, ("space", "dp")),
        P(),
    )
    out_specs = (
        P("groups", "dp", "space", None),
        P("groups", "dp", "space", None),
        P("groups", ("space", "dp")),
    )
    return jax.shard_map(
        block, mesh=mesh, in_specs=in_specs, out_specs=out_specs, check_vma=False
    )
```
